32 devices in a mesh: lon: 8 (over y, x, core), lat: 4 (over z).
Axes of the slice: x: 2, y: 2, z: 4, core: 2. Of those that a mesh axis runs over, the one named last changes fastest.
Arguments:
- background: float32 [5, 32, 128, 1024], P(None, None, 'lat', 'lon'), may hold values from -6 to 6
- velocity: float32 [2, 32, 128, 1024], P(None, None, 'lat', 'lon'), may hold values from -0.22 to 0.22
- diffusivity: float32 [5], replicated, may hold values from 0.02 to 0.12
- obs_value: float32 [32768], P(('lon', 'lat')), may hold values from -6 to 6
- obs_weight: float32 [32768], P(('lon', 'lat')), may hold values from 0.25 to 4
- obs_owner: int32 [32768, 1], P(('lon', 'lat')), may hold values from 0 to 31; in each aligned block of 1024 rows (0 to 1023, 1024 to 2047, ...) at most 64 rows name the same one
- obs_counts: int32 [32, 8], P(('lon', 'lat')), may hold values from 1 to 128, 768 in all within a row
- obs_cell: int32 [32768], P(('lon', 'lat')), may hold values from 0 to 655359
Outputs:
- forecast: float32 [5, 32, 128, 1024], P(None, None, 'lat', 'lon')
- adjoint_state: float32 [5, 32, 128, 1024], P(None, None, 'lat', 'lon')
- departures: float32 [32768], P(('lon', 'lat'))
The draws below stay inside these ranges and needn't reach their ends.
Inputs may be any that keep to these rules, and one draw needn't show every extreme that they name: `obs_owner`: among the rows of one device, padding rows included, no slab is named more than 64 times, a bound that some block reaches. `obs_counts`: each device's 8 counts sum to 768; one of them is 128. `obs_cell`: index into the owner's slab, flattened over field, level, row and longitude.
All inputs are finite; a program needn't handle non-finite values.
Results may differ from the reference program's by a relative error of at most 0.00012.
Values sent between devices are 32-bit elements; how exact they have to be, the bound alone decides.
A program may use at most 128 MiB of HBM per device.

```python
import math
import jax
import jax.numpy as jnp
import numpy as np

F = 5
K = 32
CL = 32
CW = 128
NBLK = 8
BLOCK_ROWS = 128
STEPS = 2
NLAT = 128
NLON = 1024
ROWS_DEV = 1024
OBS = 32768
CAP = 64
CELLS = 655360
N_LAT = 4
DEVICES = 32


def place_ends(values, rng, smallest, largest):
    shape = values.shape
    spot = [jax.random.randint(jax.random.fold_in(rng, axis), (), 0, shape[axis]) for axis in range(len(shape))]
    values = values.at[tuple(spot)].set(smallest)
    longest = shape.index(max(shape))
    spot[longest] = (spot[longest] + 1) % shape[longest]
    return values.at[tuple(spot)].set(largest)


def levels(rng, extent, split, low, high):
    def one(axis_at, parts):
        draws = jax.random.uniform(jax.random.fold_in(jax.random.fold_in(rng, 6), axis_at), (parts,), jnp.float32, low / len(split), high / len(split))
        return jnp.repeat(jnp.exp(draws), extent[axis_at] // parts).reshape((-1,) + (1,) * (len(extent) - axis_at - 1))

    factor_of = one(*split[0])
    for cut in split[1:]:
        factor_of = factor_of * one(*cut)
    return factor_of


def length_profile(number_of, total, bound, slope):
    portions = [(1 << 20) // math.isqrt(grade ** slope) + 1 for grade in range(2, number_of + 1)]
    spare, given = total - bound - (number_of - 1), [1] * (number_of - 1)
    while spare > 0:
        free = [i for i in range(number_of - 1) if given[i] < bound]
        mass, budget = sum([portions[i] for i in free]), spare
        for i in free:
            extra = min(bound - given[i], max(1, budget * portions[i] // mass), spare)
            given[i] = given[i] + extra
            spare = spare - extra
    return np.array([bound] + given)


def ragged(own_key, count, total, reach, slope):
    if count == 2:
        one = jax.random.randint(own_key, (), max(1, total - reach), min(reach, total - 1) + 1)
        return jnp.stack([one, total - one])
    tallies = jnp.asarray(length_profile(count, total, reach, slope), jnp.int32)
    twos = (count - 1) // 2
    source_of, taker = tallies[1:1 + 2 * twos:2], tallies[2:2 + 2 * twos:2]
    margin = jnp.minimum(source_of - 1, reach - taker)
    moved = jax.random.randint(jax.random.fold_in(own_key, 1), (twos,), 0, 1 << 20) % (margin + 1)
    tallies = tallies.at[1:1 + 2 * twos:2].set(source_of - moved).at[2:2 + 2 * twos:2].set(taker + moved)
    return tallies[jax.random.permutation(jax.random.fold_in(own_key, 2), count)]


def deal_out(stream_key, own, number, rows, amount, top, reach, skew):
    sequence = jax.random.permutation(stream_key, amount)
    packed, ordinary = portions_of(amount, rows * top, reach, skew, True), portions_of(amount, rows * top, reach, skew, False)
    places = jnp.arange(amount)

    def named(tallies, offset_by):
        used = int((tallies > 0).sum())
        fixed = max(1, used // 4)
        passed = fixed + (places - fixed + offset_by * (used - fixed)) % max(1, amount - fixed)
        return jnp.zeros((amount,), jnp.int32).at[sequence[jnp.where(places < fixed, places, passed)]].set(jnp.asarray(tallies, jnp.int32))

    tallies = jnp.where(number % 4 == 0, named(packed, number // 4), named(ordinary, number - number // 4 - 1))
    mixed = jax.random.permutation(jax.random.fold_in(own, 3), amount)
    donor, taker = mixed[0:amount // 2 * 2:2], mixed[1:amount // 2 * 2:2]
    room = jnp.minimum(tallies[donor] - 1, reach - tallies[taker]) // 2
    room = jnp.where((donor == sequence[0]) | (taker == sequence[0]) | (tallies[taker] == 0), 0, jnp.maximum(room, 0))
    passed = jax.random.randint(jax.random.fold_in(own, 4), (amount // 2,), 0, 1 << 20) % (room + 1)
    tallies = tallies.at[donor].add(-passed).at[taker].add(passed)
    items = jnp.searchsorted(jnp.cumsum(tallies), jnp.arange(rows * top), side="right").astype(jnp.int32)
    grid = items.reshape(top, rows).T
    grid = grid[jax.random.permutation(jax.random.fold_in(own, 1), rows)]
    offset_by = jax.random.randint(jax.random.fold_in(own, 2), (rows, 1), 0, top)
    return jnp.take_along_axis(grid, (jnp.arange(top)[None, :] + offset_by) % top, axis=1)


def portions_of(count, total, reach, slope, full):
    weights = [(1 << 20) // math.isqrt(rank ** slope) + 1 for rank in range(1, count + 1)]
    largest = reach if full else min(reach, max(-(-total // count), total * weights[0] // sum(weights)))
    least = 1 if total - largest >= count - 1 else 0
    given, spare = [largest] + [least] * (count - 1), total - largest - least * (count - 1)
    while spare > 0:
        candidates = [i for i in range(1, count) if given[i] < largest] or [i for i in range(1, count) if given[i] < reach]
        pool, remaining = sum([weights[i] for i in candidates]), spare
        for i in candidates:
            more = min(reach - given[i], max(1, remaining * weights[i] // pool), spare)
            given[i] = given[i] + more
            spare = spare - more
    return np.array(given)


def noise(rng, extent, scale, bound, split=(), kind=jnp.bfloat16):
    drawn = jax.random.normal(rng, extent, jnp.float32) * scale
    if len(split) > 0:
        drawn = levels(rng, extent, split, -0.22, 0.18) * drawn
    return jnp.clip(drawn, min=-bound, max=bound).astype(kind)


def setup_inputs(seed: int = 0) -> dict:
    seeds = jax.random.split(jax.random.key(seed), 9)
    background = noise(seeds[0], (F, K, NLAT, NLON), 1.0, 6.0, ((2, 4), (3, 8)), jnp.float32)
    velocity = jnp.clip(jax.random.uniform(seeds[1], (2, K, NLAT, NLON), jnp.float32, -0.22, 0.22) * levels(seeds[1], (2, K, NLAT, NLON), ((2, 4), (3, 8)), -0.4, 0.0), -0.22, 0.22)
    diffusivity = jnp.clip(jnp.exp(jax.random.uniform(seeds[2], (F,), jnp.float32, math.log(0.02), math.log(0.12))), 0.02, 0.12)
    obs_value = noise(seeds[3], (OBS,), 1.0, 6.0, ((0, 32),), jnp.float32)
    obs_weight = jnp.clip(jnp.exp(math.log(4.0) - 2.7725887 * jax.random.uniform(seeds[4], (OBS,), jnp.float32) ** levels(seeds[4], (OBS,), ((0, 32),), -0.2, 0.2)), 0.25, 4.0)
    obs_owner_keys = jax.random.split(jax.random.fold_in(seeds[5], 1), OBS // ROWS_DEV)
    obs_owner_turns = jax.random.permutation(jax.random.fold_in(seeds[5], 3), OBS // ROWS_DEV)
    obs_owner = jax.vmap(lambda own, number: deal_out(jax.random.fold_in(seeds[5], 2), own, number, ROWS_DEV, DEVICES, 1, CAP, 2))(obs_owner_keys, obs_owner_turns).reshape((OBS, 1))
    obs_counts = jax.vmap(lambda own: ragged(own, NBLK, 96 * NBLK, BLOCK_ROWS, 1))(jax.random.split(seeds[6], DEVICES)).reshape((DEVICES, NBLK)).astype(jnp.int32)
    obs_cell = place_ends(jax.random.randint(seeds[7], (OBS,), 0, CELLS), jax.random.fold_in(seeds[7], 1), 0, CELLS - 1).astype(jnp.int32)
    return {"background": background, "velocity": velocity, "diffusivity": diffusivity, "obs_value": obs_value, "obs_weight": obs_weight, "obs_owner": obs_owner, "obs_counts": obs_counts, "obs_cell": obs_cell}


FLIP_SIGNS = (1.0, 1.0, -1.0, -1.0, 1.0)


def neighbours(field, flip):
    from_east = jnp.roll(field, -1, axis=-1)
    from_west = jnp.roll(field, 1, axis=-1)
    from_south = jnp.concatenate([jnp.zeros_like(field[..., :1, :]), field[..., :-1, :]], axis=-2)
    from_north = jnp.concatenate([field[..., 1:, :], flip * field[..., -1:, ::-1]], axis=-2)
    return from_west, from_east, from_south, from_north


def reference(background, velocity, diffusivity, obs_value, obs_weight, obs_owner, obs_counts, obs_cell):
    flip = jnp.array(FLIP_SIGNS, dtype=jnp.float32)[:, None, None, None]
    eastward = velocity[0]
    northward = velocity[1]
    diffuse = diffusivity[:, None, None, None]
    centre = 1.0 - 4.0 * diffuse - jnp.abs(eastward) - jnp.abs(northward)

    def forward_step(field):
        from_west, from_east, from_south, from_north = neighbours(field, flip)
        return (centre * field + (diffuse - jnp.minimum(eastward, 0.0)) * from_east
                + (diffuse + jnp.maximum(eastward, 0.0)) * from_west
                + (diffuse - jnp.minimum(northward, 0.0)) * from_north
                + (diffuse + jnp.maximum(northward, 0.0)) * from_south)

    east_at_west, east_at_east, _, _ = neighbours(eastward, 1.0)
    _, _, north_at_south, north_at_north = neighbours(northward, 1.0)
    upper = jnp.concatenate([jnp.maximum(north_at_north[:, :-1, :], 0.0),
                             -jnp.minimum(north_at_north[:, -1:, :], 0.0)], axis=1)

    def adjoint_step(adjoint):
        from_west, from_east, from_south, from_north = neighbours(adjoint, flip)
        return (centre * adjoint + (diffuse - jnp.minimum(east_at_west, 0.0)) * from_west
                + (diffuse + jnp.maximum(east_at_east, 0.0)) * from_east
                + (diffuse - jnp.minimum(north_at_south, 0.0)) * from_south
                + (diffuse + upper) * from_north)

    states = [background]
    for step in range(STEPS):
        states.append(forward_step(states[-1]))

    all_rows = obs_value.shape[0]
    row_index = jnp.arange(all_rows, dtype=jnp.int32)
    device_of = row_index // ROWS_DEV
    local_row = row_index % ROWS_DEV
    block_index = local_row // BLOCK_ROWS
    position = local_row % BLOCK_ROWS
    is_live = position < obs_counts[device_of, block_index]
    obs_time = block_index % (STEPS + 1)
    owner_id = obs_owner[:, 0]
    field_of = obs_cell // (K * CL * CW)
    level_of = (obs_cell // (CL * CW)) % K
    row_of = (obs_cell // CW) % CL
    column_of = obs_cell % CW
    global_row = (owner_id % N_LAT) * CL + row_of
    global_column = (owner_id // N_LAT) * CW + column_of
    flat_index = ((field_of * K + level_of) * NLAT + global_row) * NLON + global_column
    flat_index = flat_index.astype(jnp.int32)
    modelled = jnp.zeros(obs_value.shape, dtype=jnp.float32)
    for step in range(STEPS + 1):
        modelled = jnp.where(obs_time == step, states[step].reshape(-1)[flat_index], modelled)
    weight = jnp.where(is_live, obs_weight, 0.0)
    departure = weight * (obs_value - modelled)
    total_cells = background.size

    def forcing(step):
        spread = jax.ops.segment_sum(jnp.where(obs_time == step, departure, 0.0), flat_index,
                                     num_segments=total_cells)
        return spread.reshape(background.shape)

    adjoint = forcing(STEPS)
    for step in range(STEPS - 1, -1, -1):
        adjoint = adjoint_step(adjoint) + forcing(step)
    return states[-1], adjoint, departure
```

```python
import functools

import jax
import jax.numpy as jnp
from jax import lax
from jax.experimental import pallas as pl
from jax.experimental.pallas import tpu as pltpu
from jax.sharding import PartitionSpec as P

STEPS = 2
FLIP_SIGNS = (1.0, 1.0, -1.0, -1.0, 1.0)
LANES = 128
TILE = 8
MESH = pl.DeviceIdType.MESH
VMEM_BYTES = 56 * 1024 * 1024
f32 = jnp.float32
bf16 = jnp.bfloat16
i32 = jnp.int32


def rows_of(start, size):
    return pl.ds(pl.multiple_of(start, size), size)


def iotas(shape):
    return lax.broadcasted_iota(i32, shape, 0), lax.broadcasted_iota(i32, shape, 1)


def parts3(x):
    one = x.astype(bf16)
    rest = x - one.astype(f32)
    two = rest.astype(bf16)
    three = (rest - two.astype(f32)).astype(bf16)
    return [one, two, three]


def as_column(row):
    return jnp.broadcast_to(row, (LANES, LANES)).T


class Place:
    def __init__(self, nlon, nlat):
        self.nlon, self.nlat = nlon, nlat
        self.devices = nlon * nlat
        self.lon = lax.axis_index("lon")
        self.lat = lax.axis_index("lat")
        self.me = self.lon * nlat + self.lat
        self.top = self.lat == nlat - 1
        self.bottom = self.lat == 0

    def peer(self, device):
        return (device // self.nlat, lax.rem(device, self.nlat))

    def hello(self):
        barrier = pltpu.get_barrier_semaphore()

        def greet(i, carry):
            other = lax.rem(self.me + i, self.devices)
            pl.semaphore_signal(barrier, inc=1, device_id=self.peer(other), device_id_type=MESH)
            return carry

        lax.fori_loop(1, self.devices, greet, 0)

    def hello_wait(self):
        pl.semaphore_wait(pltpu.get_barrier_semaphore(), self.devices - 1)


class Halo:
    def __init__(self, place, send, recv, send_sem, recv_sem):
        self.place, self.send, self.recv = place, send, recv
        p = place
        west = (lax.rem(p.lon + p.nlon - 1, p.nlon), p.lat)
        east = (lax.rem(p.lon + 1, p.nlon), p.lat)

        def copy(src, dst, k, to):
            return pltpu.make_async_remote_copy(
                src_ref=self.send[src],
                dst_ref=self.recv[dst],
                send_sem=send_sem.at[k],
                recv_sem=recv_sem.at[k],
                device_id=to,
                device_id_type=MESH,
            )

        self.to_west = copy(0, 1, 0, west)
        self.to_east = copy(1, 0, 1, east)
        self.to_south = copy(2, 3, 2, (p.lon, jnp.maximum(p.lat - 1, 0)))
        self.to_north = copy(3, 2, 3, (p.lon, jnp.minimum(p.lat + 1, p.nlat - 1)))
        self.to_fold = copy(3, 3, 4, (p.nlon - 1 - p.lon, p.lat))

    def pack_ns(self, ref, at, count, nrow):
        self.send[2][at : at + count, :] = ref[pl.ds(0, count, stride=nrow), :]
        self.send[3][at : at + count, :] = ref[pl.ds(nrow - 1, count, stride=nrow), :]

    def pack_ew(self, ref, at, blocks):
        def body(t, carry):
            turned = ref[rows_of(t * LANES, LANES), :].T
            self.send[0][pl.ds(at + t, 1), :] = turned[0:1, :]
            self.send[1][pl.ds(at + t, 1), :] = turned[LANES - 1 : LANES, :]
            return carry

        lax.fori_loop(0, blocks, body, 0)

    def start(self):
        p = self.place
        self.to_west.start()
        self.to_east.start()

        @pl.when(jnp.logical_not(p.bottom))
        def _():
            self.to_south.start()

        @pl.when(jnp.logical_not(p.top))
        def _():
            self.to_north.start()

        @pl.when(p.top)
        def _():
            self.to_fold.start()

    def wait(self):
        p = self.place
        self.to_west.wait()
        self.to_east.wait()

        @pl.when(jnp.logical_not(p.bottom))
        def _():
            self.to_south.wait_send()
            self.to_north.wait_recv()

        @pl.when(p.bottom)
        def _():
            self.recv[2][...] = jnp.zeros_like(self.recv[2])

        @pl.when(jnp.logical_not(p.top))
        def _():
            self.to_north.wait_send()
            self.to_south.wait_recv()

        @pl.when(p.top)
        def _():
            self.to_fold.wait()

    def finish_north(self, nfield, nlevel, extra):
        raw = self.recv[3][...]
        i, j = iotas((LANES, LANES))
        turn = (i + j == LANES - 1).astype(bf16)
        a, b, c = [jnp.dot(x, turn, preferred_element_type=f32) for x in parts3(raw)]
        mirrored = (a + b) + c
        signs = [FLIP_SIGNS[k] for k in range(nfield)] + ([-1.0] if extra else [])
        for k, sign in enumerate(signs):
            part = slice(k * nlevel, (k + 1) * nlevel)
            self.recv[3][part, :] = jnp.where(self.place.top, sign * mirrored[part], raw[part])


def unpack_ew(west, east, t):
    i, _ = iotas((LANES, LANES))
    w = west[pl.ds(t, 1), :]
    e = east[pl.ds(t, 1), :]
    return jnp.where(i == 0, w, jnp.where(i == LANES - 1, e, 0.0)).T


def shifted(x, z, south, north):
    nrow = x.shape[0]
    i, j = iotas(x.shape)
    return (
        jnp.where(j == 0, z, pltpu.roll(x, 1, 1)),
        jnp.where(j == LANES - 1, z, pltpu.roll(x, LANES - 1, 1)),
        jnp.where(i == 0, south, pltpu.roll(x, 1, 0)),
        jnp.where(i == nrow - 1, north, pltpu.roll(x, nrow - 1, 0)),
    )


def step_loop(dims, recv, edge, body):
    nfield, nlevel, nrow = dims
    per = LANES // nrow
    west, east, south, north = recv

    def group(q, carry):
        for f in range(nfield):
            t = f * (nlevel // per) + q
            edge[f * LANES : (f + 1) * LANES, :] = unpack_ew(west, east, t)
        for i in range(per):
            level = q * per + i
            halos = []
            for f in range(nfield):
                z = edge[f * LANES + i * nrow : f * LANES + (i + 1) * nrow, :]
                row = f * nlevel + level
                halos.append((z, south[pl.ds(row, 1), :], north[pl.ds(row, 1), :]))
            body(level, halos)
        return carry

    lax.fori_loop(0, nlevel // per, group, 0)


def forward_step(dims, src, dst, vel, kap, recv, edge):
    nfield, nlevel, nrow = dims

    def body(level, halos):
        u = vel[rows_of(level * nrow, nrow), :]
        v = vel[rows_of((nlevel + level) * nrow, nrow), :]
        speed_u, speed_v = jnp.abs(u), jnp.abs(v)
        for f in range(nfield):
            at = rows_of((f * nlevel + level) * nrow, nrow)
            x = src[at, :]
            w, e, s, n = shifted(x, *halos[f])
            dst[at, :] = (
                x
                + kap[f] * (((e + w) + (n + s)) - 4.0 * x)
                + speed_u * (jnp.where(u < 0.0, e, w) - x)
                + speed_v * (jnp.where(v < 0.0, n, s) - x)
            )

    step_loop(dims, recv, edge, body)


def adjoint_step(dims, src, add, dst, vel, coefs, kap, recv, edge):
    nfield, nlevel, nrow = dims
    cw, ce, cs, cn = coefs

    def body(level, halos):
        here = rows_of(level * nrow, nrow)
        u = vel[here, :]
        v = vel[rows_of((nlevel + level) * nrow, nrow), :]
        keep = 1.0 - jnp.abs(u) - jnp.abs(v)
        lw, le, ls, ln = cw[here, :], ce[here, :], cs[here, :], cn[here, :]
        for f in range(nfield):
            at = rows_of((f * nlevel + level) * nrow, nrow)
            x = src[at, :]
            w, e, s, n = shifted(x, *halos[f])
            dst[at, :] = (
                (keep * x + add[at, :])
                + kap[f] * (((e + w) + (n + s)) - 4.0 * x)
                + (lw * w + le * e)
                + (ls * s + ln * n)
            )

    step_loop(dims, recv, edge, body)


def live_onehot(owner, counts, b, devices):
    i, j = iotas((devices, LANES))
    return jnp.where((owner[b : b + 1, :] == i) & (j < counts[0, b]), 1.0, 0.0).astype(f32)


def exchange_copy(place, i, src, dst, send_sem, recv_sem):
    return pltpu.make_async_remote_copy(
        src_ref=src,
        dst_ref=dst,
        send_sem=send_sem.at[i],
        recv_sem=recv_sem.at[i],
        device_id=place.peer(lax.rem(place.me + i, place.devices)),
        device_id_type=MESH,
    )


def tile_at(ref, index):
    return ref.at[rows_of(index * TILE, TILE), :]


def kernel_forward(
    nlon, nlat, dims, cap, owner, counts, kap, x0, vel, value, weight, cell,
    x1, x2, cw, ce, cs, cn, slots, got,
    sw, se, ss, sn, rw, re, rs, rn, sw2, se2, ss2, sn2, rw2, re2, rs2, rn2,
    edge, packed, landed, halo_send, halo_recv, row_send, row_recv,
):
    nfield, nlevel, nrow = dims
    place = Place(nlon, nlat)
    devices = place.devices
    nfk = nfield * nlevel
    blocks = nfk * nrow // LANES
    vblocks = nlevel * nrow // LANES
    place.hello()
    first = Halo(place, (sw, se, ss, sn), (rw, re, rs, rn), halo_send.at[0], halo_recv.at[0])
    first.pack_ns(x0, 0, nfk, nrow)
    first.pack_ns(vel.at[pl.ds(nlevel * nrow, nlevel * nrow), :], nfk, nlevel, nrow)
    first.pack_ew(x0, 0, blocks)
    first.pack_ew(vel, blocks, vblocks)
    place.hello_wait()
    first.start()

    nblock = owner.shape[0]
    shared = LANES // cap
    offset = lax.rem(place.me, shared) * cap
    i, j = iotas((LANES, LANES))
    before = (i < j).astype(bf16)
    base = jnp.zeros((devices, 1), f32)
    total = None
    for b in range(nblock):
        onehot = live_onehot(owner, counts, b, devices)
        earlier = jnp.dot(onehot.astype(bf16), before, preferred_element_type=f32)
        slot = jnp.sum(onehot * (earlier + base), axis=0, keepdims=True)
        base = base + jnp.sum(onehot, axis=1, keepdims=True)
        slots[b : b + 1, :] = slot
        code = ((b % (STEPS + 1)) * nfk * nrow * LANES + cell[b : b + 1, :]).astype(f32)
        stack = []
        for data in (value[b : b + 1, :], weight[b : b + 1, :], code):
            stack += parts3(onehot * data)
        place_of = as_column(slot).astype(i32) + offset
        put = (place_of == j).astype(bf16)
        out = jnp.dot(jnp.concatenate(stack, axis=0), put, preferred_element_type=f32)
        total = out if total is None else total + out
    for c in range(3):
        a = total[(3 * c) * devices : (3 * c + 1) * devices]
        a = a + total[(3 * c + 1) * devices : (3 * c + 2) * devices]
        a = a + total[(3 * c + 2) * devices : (3 * c + 3) * devices]
        packed[pl.ds(c, devices, stride=TILE), :] = a
    _, lane = iotas((devices, LANES))
    mine = (lane >= offset) & (lane < offset + cap)
    tally = jnp.where(mine, base, 0.0)
    for c in range(3, TILE):
        packed[pl.ds(c, devices, stride=TILE), :] = tally

    def send_row(i, carry):
        target = lax.rem(place.me + i, devices)
        exchange_copy(
            place, i, tile_at(packed, target), tile_at(landed, place.me), row_send, row_recv
        ).start()
        return carry

    lax.fori_loop(1, devices, send_row, 0)
    landed[rows_of(place.me * TILE, TILE), :] = packed[rows_of(place.me * TILE, TILE), :]

    first.wait()
    first.finish_north(nfield, nlevel, True)
    forward_step(dims, x0, x1, vel, kap, first.recv, edge)
    second = Halo(
        place, (sw2, se2, ss2, sn2), (rw2, re2, rs2, rn2), halo_send.at[1], halo_recv.at[1]
    )
    second.pack_ns(x1, 0, nfk, nrow)
    second.pack_ew(x1, 0, blocks)
    second.start()

    per = LANES // nrow

    def coefficients(q, carry):
        z = unpack_ew(rw, re, blocks + q)
        for k in range(per):
            level = q * per + k
            here = rows_of(level * nrow, nrow)
            row = nfk + level
            zero = jnp.zeros((1, LANES), f32)
            u = vel[here, :]
            v = vel[rows_of((nlevel + level) * nrow, nrow), :]
            uw, ue, _, _ = shifted(u, z[k * nrow : (k + 1) * nrow], zero, zero)
            _, _, vs, vn = shifted(v, v, rs[pl.ds(row, 1), :], rn[pl.ds(row, 1), :])
            cw[here, :] = -jnp.minimum(uw, 0.0)
            ce[here, :] = jnp.maximum(ue, 0.0)
            cs[here, :] = -jnp.minimum(vs, 0.0)
            cn[here, :] = jnp.maximum(vn, 0.0)
        return carry

    lax.fori_loop(0, nlevel // per, coefficients, 0)
    second.wait()
    second.finish_north(nfield, nlevel, False)
    forward_step(dims, x1, x2, vel, kap, second.recv, edge)

    def wait_row(i, carry):
        source = lax.rem(place.me + devices - i, devices)
        copy = exchange_copy(
            place, i, tile_at(packed, place.me), tile_at(landed, source), row_send, row_recv
        )
        copy.wait_recv()
        copy.wait_send()
        return carry

    lax.fori_loop(1, devices, wait_row, 0)
    got[...] = landed[...]


def kernel_rows(
    devices, cap, x0, x1, x2, got, forcing, back,
    states, picked, tiles, code_v, tally_v, code_s, tally_s, sems,
):
    cells = x0.shape[0]
    shared = LANES // cap
    groups = devices // shared
    loads = []
    for k, x in enumerate((x0, x1, x2)):
        load = pltpu.make_async_copy(x, states.at[pl.ds(k * cells, cells), :], sems.at[k])
        load.start()
        loads.append(load)
    for g in range(groups):
        tile = got[g * shared * TILE : (g * shared + 1) * TILE, :]
        for k in range(1, shared):
            tile = tile + got[(g * shared + k) * TILE : (g * shared + k + 1) * TILE, :]
        tiles[g * TILE : (g + 1) * TILE, :] = tile
        code_v[g : g + 1, :] = tile[2:3, :].astype(i32)
        tally_v[g : g + 1, :] = tile[3:4, :].astype(i32)
    codes = pltpu.make_async_copy(code_v, code_s, sems.at[3])
    tallies = pltpu.make_async_copy(tally_v, tally_s, sems.at[4])
    codes.start()
    tallies.start()

    def clear(i, carry):
        forcing[rows_of(i * LANES, LANES), :] = jnp.zeros((LANES, LANES), f32)
        return carry

    lax.fori_loop(0, forcing.shape[0] // LANES, clear, 0)
    codes.wait()
    tallies.wait()
    for load in loads:
        load.wait()

    def over_rows(visit):
        def source(s, carry):
            g = s // shared
            at = lax.rem(s, shared) * cap

            def chunk(c, inner):
                for k in range(TILE):
                    lane = at + c * TILE + k
                    visit(lax.shift_right_logical(code_s[g, lane], 7), g * LANES + lane)
                return inner

            lax.fori_loop(0, (tally_s[g, at] + TILE - 1) // TILE, chunk, 0)
            return carry

        lax.fori_loop(0, devices, source, 0)

    def pick(row, slot):
        picked[pl.ds(slot, 1), :] = states[pl.ds(row, 1), :]

    over_rows(pick)

    def departures(g, carry):
        at = rows_of(g * TILE, TILE)
        tile = tiles[at, :]
        _, j = iotas((LANES, LANES))
        weight = as_column(tile[1:2, :])
        lane = as_column(jnp.bitwise_and(tile[2:3, :].astype(i32), LANES - 1).astype(f32))
        here = rows_of(g * LANES, LANES)
        row = weight * (as_column(tile[0:1, :]) - picked[here, :])
        row = jnp.where((lane.astype(i32) == j) & (weight != 0.0), row, 0.0)
        picked[here, :] = row
        back[at, :] = jnp.broadcast_to(jnp.sum(row.T, axis=0, keepdims=True), (TILE, LANES))
        return carry

    lax.fori_loop(0, groups, departures, 0)

    def spread(row, slot):
        at = pl.ds(row, 1)
        forcing[at, :] = forcing[at, :] + picked[pl.ds(slot, 1), :]

    over_rows(spread)


def kernel_adjoint(
    nlon, nlat, dims, cap, owner, counts, kap, forcing, vel, cw, ce, cs, cn, slots, back,
    adjoint, departures,
    sw, se, ss, sn, rw, re, rs, rn, sw2, se2, ss2, sn2, rw2, re2, rs2, rn2,
    edge, middle, landed, halo_send, halo_recv, row_send, row_recv,
):
    nfield, nlevel, nrow = dims
    place = Place(nlon, nlat)
    devices = place.devices
    nfk = nfield * nlevel
    rows = nfk * nrow
    blocks = rows // LANES
    shared = LANES // cap
    coefs = (cw, ce, cs, cn)
    part = [forcing.at[pl.ds(k * rows, rows), :] for k in range(STEPS + 1)]
    place.hello()
    first = Halo(place, (sw, se, ss, sn), (rw, re, rs, rn), halo_send.at[0], halo_recv.at[0])
    first.pack_ns(part[2], 0, nfk, nrow)
    first.pack_ew(part[2], 0, blocks)
    place.hello_wait()
    first.start()

    def send_row(i, carry):
        target = lax.rem(place.me + i, devices)
        exchange_copy(
            place, i, tile_at(back, target // shared), tile_at(landed, place.me), row_send, row_recv
        ).start()
        return carry

    lax.fori_loop(1, devices, send_row, 0)
    landed[rows_of(place.me * TILE, TILE), :] = back[rows_of((place.me // shared) * TILE, TILE), :]

    first.wait()
    first.finish_north(nfield, nlevel, False)
    adjoint_step(dims, part[2], part[1], middle, vel, coefs, kap, first.recv, edge)
    second = Halo(
        place, (sw2, se2, ss2, sn2), (rw2, re2, rs2, rn2), halo_send.at[1], halo_recv.at[1]
    )
    second.pack_ns(middle, 0, nfk, nrow)
    second.pack_ew(middle, 0, blocks)
    second.start()

    def wait_row(i, carry):
        source = lax.rem(place.me + devices - i, devices)
        copy = exchange_copy(
            place, i, tile_at(back, 0), tile_at(landed, source), row_send, row_recv
        )
        copy.wait_recv()
        copy.wait_send()
        return carry

    lax.fori_loop(1, devices, wait_row, 0)
    offset = lax.rem(place.me, shared) * cap
    stack = jnp.concatenate(parts3(landed[pl.ds(0, devices, stride=TILE), :]), axis=0)
    i, _ = iotas((LANES, LANES))
    for b in range(owner.shape[0]):
        take = (slots[b : b + 1, :].astype(i32) + offset == i).astype(bf16)
        out = jnp.dot(stack, take, preferred_element_type=f32)
        out = (out[:devices] + out[devices : 2 * devices]) + out[2 * devices :]
        onehot = live_onehot(owner, counts, b, devices)
        departures[b : b + 1, :] = jnp.sum(onehot * out, axis=0, keepdims=True)

    second.wait()
    second.finish_north(nfield, nlevel, False)
    adjoint_step(dims, middle, part[0], adjoint, vel, coefs, kap, second.recv, edge)


def vmem(*shape):
    return jax.ShapeDtypeStruct(shape, f32)


def shards(
    nlon, nlat,
    background, velocity, diffusivity, obs_value, obs_weight, obs_owner, obs_counts, obs_cell,
):
    devices = nlon * nlat
    nfield, nlevel, nrow, ncolumn = background.shape
    nfk = nfield * nlevel
    rows = nfk * nrow
    dims = (nfield, nlevel, nrow)
    nobs = obs_value.shape[0]
    cap = 2 * nobs // devices
    nblock = obs_counts.shape[1]
    blocks = rows // LANES
    vblocks = nlevel * nrow // LANES
    groups = devices * cap // LANES
    x0 = background.reshape(rows, LANES)
    vel = velocity.reshape(2 * nlevel * nrow, LANES)
    owner = obs_owner.reshape(nblock, LANES)
    value, weight, cell = [a.reshape(nblock, LANES) for a in (obs_value, obs_weight, obs_cell)]
    in_vmem = pl.BlockSpec(memory_space=pltpu.VMEM)
    in_smem = pl.BlockSpec(memory_space=pltpu.SMEM)
    anywhere = pl.BlockSpec(memory_space=pl.ANY)

    def halo_scratch(ew, ns):
        return [pltpu.VMEM((ew, LANES), f32)] * 2 + [pltpu.VMEM((ns, LANES), f32)] * 2

    sems = [
        pltpu.SemaphoreType.DMA((2, 5)),
        pltpu.SemaphoreType.DMA((2, 5)),
        pltpu.SemaphoreType.DMA((devices,)),
        pltpu.SemaphoreType.DMA((devices,)),
    ]
    small = halo_scratch(blocks, nfk)
    large = halo_scratch(blocks + vblocks, nfk + nlevel)
    edge = pltpu.VMEM((nfield * LANES, LANES), f32)
    tiles = pltpu.VMEM((devices * TILE, LANES), f32)
    level_rows = nlevel * nrow

    x1, x2, cw, ce, cs, cn, slots, got = pl.pallas_call(
        functools.partial(kernel_forward, nlon, nlat, dims, cap),
        out_shape=[vmem(rows, LANES)] * 2
        + [vmem(level_rows, LANES)] * 4
        + [vmem(nblock, LANES), vmem(devices * TILE, LANES)],
        in_specs=[in_vmem, in_smem, in_smem] + [in_vmem] * 5,
        out_specs=[in_vmem] * 8,
        scratch_shapes=large + large + small + small + [edge, tiles, tiles] + sems,
        compiler_params=pltpu.CompilerParams(
            collective_id=0, has_side_effects=True, vmem_limit_bytes=VMEM_BYTES
        ),
        name="forward",
    )(owner, obs_counts, diffusivity, x0, vel, value, weight, cell)

    forcing, back = pl.pallas_call(
        functools.partial(kernel_rows, devices, cap),
        out_shape=[vmem((STEPS + 1) * rows, LANES), vmem(groups * TILE, LANES)],
        in_specs=[anywhere] * 3 + [in_vmem],
        out_specs=[in_vmem] * 2,
        scratch_shapes=[
            pltpu.VMEM(((STEPS + 1) * rows, LANES), f32),
            pltpu.VMEM((groups * LANES, LANES), f32),
            pltpu.VMEM((groups * TILE, LANES), f32),
            pltpu.VMEM((groups, LANES), i32),
            pltpu.VMEM((groups, LANES), i32),
            pltpu.SMEM((groups, LANES), i32),
            pltpu.SMEM((groups, LANES), i32),
            pltpu.SemaphoreType.DMA((5,)),
        ],
        compiler_params=pltpu.CompilerParams(vmem_limit_bytes=VMEM_BYTES),
        name="rows",
    )(x0, x1, x2, got)

    adjoint, departures = pl.pallas_call(
        functools.partial(kernel_adjoint, nlon, nlat, dims, cap),
        out_shape=[vmem(rows, LANES), vmem(nblock, LANES)],
        in_specs=[in_vmem, in_smem, in_smem] + [in_vmem] * 8,
        out_specs=[in_vmem] * 2,
        scratch_shapes=small * 4
        + [edge, pltpu.VMEM((rows, LANES), f32), tiles]
        + sems,
        compiler_params=pltpu.CompilerParams(
            collective_id=1, has_side_effects=True, vmem_limit_bytes=VMEM_BYTES
        ),
        name="adjoint",
    )(owner, obs_counts, diffusivity, forcing, vel, cw, ce, cs, cn, slots, back)

    shape = background.shape
    return x2.reshape(shape), adjoint.reshape(shape), departures.reshape(nobs)


def solution(mesh):
    in_specs = (
        P(None, None, "lat", "lon"),
        P(None, None, "lat", "lon"),
        P(),
        P(("lon", "lat")),
        P(("lon", "lat")),
        P(("lon", "lat"), None),
        P(("lon", "lat"), None),
        P(("lon", "lat")),
    )
    out_specs = (P(None, None, "lat", "lon"), P(None, None, "lat", "lon"), P(("lon", "lat")))
    inner = functools.partial(shards, mesh.shape["lon"], mesh.shape["lat"])
    return jax.shard_map(inner, mesh=mesh, in_specs=in_specs, out_specs=out_specs, check_vma=False)
```

```python
import functools

import jax
import jax.numpy as jnp
from jax import lax
from jax.experimental import pallas as pl
from jax.experimental.pallas import tpu as pltpu
from jax.sharding import PartitionSpec as P

STEPS = 2
FLIP_SIGNS = (1.0, 1.0, -1.0, -1.0, 1.0)
LANES = 128
TILE = 8
GROUP = 64
MESH = pl.DeviceIdType.MESH
VMEM_BYTES = 56 * 1024 * 1024
f32 = jnp.float32
bf16 = jnp.bfloat16
i32 = jnp.int32


def rows_of(start, size):
    return pl.ds(pl.multiple_of(start, size), size)


def iotas(shape):
    return lax.broadcasted_iota(i32, shape, 0), lax.broadcasted_iota(i32, shape, 1)


def parts3(x):
    one = x.astype(bf16)
    rest = x - one.astype(f32)
    two = rest.astype(bf16)
    three = (rest - two.astype(f32)).astype(bf16)
    return [one, two, three]


def as_column(row):
    return jnp.broadcast_to(row, (LANES, LANES)).T


class Place:
    def __init__(self, nlon, nlat):
        self.nlon, self.nlat = nlon, nlat
        self.devices = nlon * nlat
        self.lon = lax.axis_index("lon")
        self.lat = lax.axis_index("lat")
        self.me = self.lon * nlat + self.lat
        self.top = self.lat == nlat - 1
        self.bottom = self.lat == 0

    def peer(self, device):
        return (device // self.nlat, lax.rem(device, self.nlat))

    def hello(self):
        barrier = pltpu.get_barrier_semaphore()

        def greet(i, carry):
            other = lax.rem(self.me + i, self.devices)
            pl.semaphore_signal(barrier, inc=1, device_id=self.peer(other), device_id_type=MESH)
            return carry

        lax.fori_loop(1, self.devices, greet, 0)

    def hello_wait(self):
        pl.semaphore_wait(pltpu.get_barrier_semaphore(), self.devices - 1)


class Halo:
    def __init__(self, place, send, recv, send_sem, recv_sem):
        self.place, self.send, self.recv = place, send, recv
        p = place
        west = (lax.rem(p.lon + p.nlon - 1, p.nlon), p.lat)
        east = (lax.rem(p.lon + 1, p.nlon), p.lat)

        def copy(src, dst, k, to):
            return pltpu.make_async_remote_copy(
                src_ref=self.send[src],
                dst_ref=self.recv[dst],
                send_sem=send_sem.at[k],
                recv_sem=recv_sem.at[k],
                device_id=to,
                device_id_type=MESH,
            )

        self.to_west = copy(0, 1, 0, west)
        self.to_east = copy(0, 0, 1, east)
        self.to_south = copy(1, 3, 2, (p.lon, jnp.maximum(p.lat - 1, 0)))
        self.to_north = copy(2, 2, 3, (p.lon, jnp.minimum(p.lat + 1, p.nlat - 1)))
        self.to_fold = copy(2, 3, 4, (p.nlon - 1 - p.lon, p.lat))

    def pack_ns(self, ref, at, count, nrow):
        self.send[1][at : at + count, :] = ref[pl.ds(0, count, stride=nrow), :]
        self.send[2][at : at + count, :] = ref[pl.ds(nrow - 1, count, stride=nrow), :]

    def pack_ew(self, ref, at, tiles):
        _, j = iotas((TILE, LANES))
        owner = jnp.bitwise_and(lax.shift_right_logical(j + 1, 1), GROUP - 1)

        def body(t, carry):
            total = jnp.zeros((TILE, LANES), f32)
            for m in range(GROUP):
                x = ref[rows_of(t * GROUP * TILE + m * TILE, TILE), :]
                x = pltpu.roll(x, 2 * m, 1) if m else x
                total = jnp.where(owner == m, x, total)
            self.send[0][rows_of((at + t) * TILE, TILE), :] = total
            return carry

        lax.fori_loop(0, tiles, body, 0)

    def start(self):
        p = self.place
        self.to_west.start()
        self.to_east.start()

        @pl.when(jnp.logical_not(p.bottom))
        def _():
            self.to_south.start()

        @pl.when(jnp.logical_not(p.top))
        def _():
            self.to_north.start()

        @pl.when(p.top)
        def _():
            self.to_fold.start()

    def wait(self):
        p = self.place
        self.to_west.wait()
        self.to_east.wait()

        @pl.when(jnp.logical_not(p.bottom))
        def _():
            self.to_south.wait_send()
            self.to_north.wait_recv()

        @pl.when(p.bottom)
        def _():
            self.recv[2][...] = jnp.zeros_like(self.recv[2])

        @pl.when(jnp.logical_not(p.top))
        def _():
            self.to_north.wait_send()
            self.to_south.wait_recv()

        @pl.when(p.top)
        def _():
            self.to_fold.wait()

    def finish(self, nfield, nlevel, extra):
        west, east = self.recv[0][...], self.recv[1][...]
        _, j = iotas(west.shape)
        odd = jnp.bitwise_and(j, 1) == 1
        self.recv[0][...] = jnp.where(odd, pltpu.roll(west, 2, 1), east)
        raw = self.recv[3][...]
        i, j = iotas((LANES, LANES))
        turn = (i + j == LANES - 1).astype(bf16)
        a, b, c = [jnp.dot(x, turn, preferred_element_type=f32) for x in parts3(raw)]
        mirrored = (a + b) + c
        signs = [FLIP_SIGNS[k] for k in range(nfield)] + ([-1.0] if extra else [])
        for k, sign in enumerate(signs):
            part = slice(k * nlevel, (k + 1) * nlevel)
            self.recv[3][part, :] = jnp.where(self.place.top, sign * mirrored[part], raw[part])

    def halos(self):
        return self.recv[0], self.recv[2], self.recv[3]


def shifted(x, halos, index, level, nlevel):
    columns, south, north = halos
    nrow = x.shape[0]
    per = nrow // TILE
    first = level * per
    tile = columns[rows_of((index * (nlevel * per // GROUP) + first // GROUP) * TILE, TILE), :]
    turn = LANES - 1 - 2 * lax.rem(first, GROUP)
    z = jnp.concatenate([pltpu.roll(tile, turn - 2 * r, 1) for r in range(per)], axis=0)
    s = south[pl.ds(index * nlevel + level, 1), :]
    n = north[pl.ds(index * nlevel + level, 1), :]
    i, j = iotas(x.shape)
    return (
        jnp.where(j == 0, z, pltpu.roll(x, 1, 1)),
        jnp.where(j == LANES - 1, z, pltpu.roll(x, LANES - 1, 1)),
        jnp.where(i == 0, s, pltpu.roll(x, 1, 0)),
        jnp.where(i == nrow - 1, n, pltpu.roll(x, nrow - 1, 0)),
    )


def forward_step(dims, src, dst, vel, kap, halos):
    nfield, nlevel, nrow = dims

    def body(level, carry):
        u = vel[rows_of(level * nrow, nrow), :]
        v = vel[rows_of((nlevel + level) * nrow, nrow), :]
        speed_u, speed_v = jnp.abs(u), jnp.abs(v)
        for f in range(nfield):
            at = rows_of((f * nlevel + level) * nrow, nrow)
            x = src[at, :]
            w, e, s, n = shifted(x, halos, f, level, nlevel)
            dst[at, :] = (
                x
                + kap[f] * (((e + w) + (n + s)) - 4.0 * x)
                + speed_u * (jnp.where(u < 0.0, e, w) - x)
                + speed_v * (jnp.where(v < 0.0, n, s) - x)
            )
        return carry

    lax.fori_loop(0, nlevel, body, 0)


def adjoint_level(dims, level, src, add, put, u, v, kap, halos, vel_halos):
    nfield, nlevel, nrow = dims
    keep = 1.0 - jnp.abs(u) - jnp.abs(v)
    uw, ue, _, _ = shifted(u, vel_halos, 0, level, nlevel)
    _, _, vs, vn = shifted(v, vel_halos, 0, level, nlevel)
    lw, le = -jnp.minimum(uw, 0.0), jnp.maximum(ue, 0.0)
    ls, ln = -jnp.minimum(vs, 0.0), jnp.maximum(vn, 0.0)
    for f in range(nfield):
        x = src(f)
        w, e, s, n = shifted(x, halos, f, level, nlevel)
        put(
            f,
            (keep * x + add(f))
            + kap[f] * (((e + w) + (n + s)) - 4.0 * x)
            + (lw * w + le * e)
            + (ls * s + ln * n),
        )


def live_onehot(owner, counts, b, devices):
    i, j = iotas((devices, LANES))
    return jnp.where((owner[b : b + 1, :] == i) & (j < counts[0, b]), 1.0, 0.0).astype(f32)


def exchange_copy(place, i, src, dst, send_sem, recv_sem):
    return pltpu.make_async_remote_copy(
        src_ref=src,
        dst_ref=dst,
        send_sem=send_sem.at[i],
        recv_sem=recv_sem.at[i],
        device_id=place.peer(lax.rem(place.me + i, place.devices)),
        device_id_type=MESH,
    )


def tile_at(ref, index):
    return ref.at[rows_of(index * TILE, TILE), :]


def kernel_forward(
    nlon, nlat, dims, cap, owner, counts, kap, x0, vel, value, weight, cell,
    x1, hc, hs, hn, vc, vs, vn, slots, got,
    sc, ss, sn, rw, re, rs, rn, sc2, ss2, sn2, rw2, re2, rs2, rn2,
    state, packed, landed, halo_send, halo_recv, row_send, row_recv, keep_sem,
):
    nfield, nlevel, nrow = dims
    place = Place(nlon, nlat)
    devices = place.devices
    nfk = nfield * nlevel
    ctiles = nfk * nrow // TILE // GROUP
    vtiles = nlevel * nrow // TILE // GROUP
    place.hello()
    first = Halo(place, (sc, ss, sn), (rw, re, rs, rn), halo_send.at[0], halo_recv.at[0])
    first.pack_ns(x0, 0, nfk, nrow)
    first.pack_ns(vel.at[pl.ds(nlevel * nrow, nlevel * nrow), :], nfk, nlevel, nrow)
    first.pack_ew(x0, 0, ctiles)
    first.pack_ew(vel, ctiles, vtiles)
    place.hello_wait()
    first.start()

    nblock = owner.shape[0]
    shared = LANES // cap
    offset = lax.rem(place.me, shared) * cap
    i, j = iotas((LANES, LANES))
    before = (i < j).astype(bf16)
    base = jnp.zeros((devices, 1), f32)
    total = None
    for b in range(nblock):
        onehot = live_onehot(owner, counts, b, devices)
        earlier = jnp.dot(onehot.astype(bf16), before, preferred_element_type=f32)
        slot = jnp.sum(onehot * (earlier + base), axis=0, keepdims=True)
        base = base + jnp.sum(onehot, axis=1, keepdims=True)
        slots[b : b + 1, :] = slot
        code = ((b % (STEPS + 1)) * nfk * nrow * LANES + cell[b : b + 1, :]).astype(f32)
        stack = []
        for data in (value[b : b + 1, :], weight[b : b + 1, :], code):
            stack += parts3(onehot * data)
        place_of = as_column(slot).astype(i32) + offset
        put = (place_of == j).astype(bf16)
        out = jnp.dot(jnp.concatenate(stack, axis=0), put, preferred_element_type=f32)
        total = out if total is None else total + out
    for c in range(3):
        a = total[(3 * c) * devices : (3 * c + 1) * devices]
        a = a + total[(3 * c + 1) * devices : (3 * c + 2) * devices]
        a = a + total[(3 * c + 2) * devices : (3 * c + 3) * devices]
        packed[pl.ds(c, devices, stride=TILE), :] = a
    _, lane = iotas((devices, LANES))
    mine = (lane >= offset) & (lane < offset + cap)
    tally = jnp.where(mine, base, 0.0)
    for c in range(3, TILE):
        packed[pl.ds(c, devices, stride=TILE), :] = tally

    def send_row(i, carry):
        target = lax.rem(place.me + i, devices)
        exchange_copy(
            place, i, tile_at(packed, target), tile_at(landed, place.me), row_send, row_recv
        ).start()
        return carry

    lax.fori_loop(1, devices, send_row, 0)
    landed[rows_of(place.me * TILE, TILE), :] = packed[rows_of(place.me * TILE, TILE), :]

    first.wait()
    first.finish(nfield, nlevel, True)
    forward_step(dims, x0, state, vel, kap, first.halos())
    second = Halo(place, (sc2, ss2, sn2), (rw2, re2, rs2, rn2), halo_send.at[1], halo_recv.at[1])
    second.pack_ns(state, 0, nfk, nrow)
    second.pack_ew(state, 0, ctiles)
    second.start()
    keep = pltpu.make_async_copy(state, x1, keep_sem)
    keep.start()
    vc[...] = rw[ctiles * TILE :, :]
    vs[...] = rs[nfk:, :]
    vn[...] = rn[nfk:, :]

    def wait_row(i, carry):
        source = lax.rem(place.me + devices - i, devices)
        copy = exchange_copy(
            place, i, tile_at(packed, place.me), tile_at(landed, source), row_send, row_recv
        )
        copy.wait_recv()
        copy.wait_send()
        return carry

    lax.fori_loop(1, devices, wait_row, 0)
    got[...] = landed[...]
    second.wait()
    second.finish(nfield, nlevel, False)
    hc[...] = rw2[...]
    hs[...] = rs2[...]
    hn[...] = rn2[...]
    keep.wait()


def kernel_rows(
    devices, dims, cap, kap, x0, x1, vel, hc, hs, hn, got, x2, forcing, back,
    states, picked, tiles, code_v, tally_v, code_s, tally_s, sems,
):
    cells = x0.shape[0]
    shared = LANES // cap
    groups = devices // shared
    loads = []
    for k, x in enumerate((x0, x1)):
        load = pltpu.make_async_copy(x, states.at[pl.ds(k * cells, cells), :], sems.at[k])
        load.start()
        loads.append(load)
    for g in range(groups):
        tile = got[g * shared * TILE : (g * shared + 1) * TILE, :]
        for k in range(1, shared):
            tile = tile + got[(g * shared + k) * TILE : (g * shared + k + 1) * TILE, :]
        tiles[g * TILE : (g + 1) * TILE, :] = tile
        code_v[g : g + 1, :] = tile[2:3, :].astype(i32)
        tally_v[g : g + 1, :] = tile[3:4, :].astype(i32)
    codes = pltpu.make_async_copy(code_v, code_s, sems.at[3])
    tallies = pltpu.make_async_copy(tally_v, tally_s, sems.at[4])
    codes.start()
    tallies.start()

    def clear(i, carry):
        forcing[rows_of(i * LANES, LANES), :] = jnp.zeros((LANES, LANES), f32)
        return carry

    lax.fori_loop(0, forcing.shape[0] // LANES, clear, 0)
    codes.wait()
    tallies.wait()
    for load in loads:
        load.wait()
    newest = states.at[pl.ds(2 * cells, cells), :]
    forward_step(dims, states.at[pl.ds(cells, cells), :], newest, vel, kap, (hc, hs, hn))
    store = pltpu.make_async_copy(newest, x2, sems.at[2])
    store.start()

    def over_rows(visit):
        def source(s, carry):
            g = s // shared
            at = lax.rem(s, shared) * cap

            def chunk(c, inner):
                for k in range(TILE):
                    lane = at + c * TILE + k
                    visit(lax.shift_right_logical(code_s[g, lane], 7), g * LANES + lane)
                return inner

            lax.fori_loop(0, (tally_s[g, at] + TILE - 1) // TILE, chunk, 0)
            return carry

        lax.fori_loop(0, devices, source, 0)

    def pick(row, slot):
        picked[pl.ds(slot, 1), :] = states[pl.ds(row, 1), :]

    over_rows(pick)

    def departures(g, carry):
        at = rows_of(g * TILE, TILE)
        tile = tiles[at, :]
        _, j = iotas((LANES, LANES))
        weight = as_column(tile[1:2, :])
        lane = as_column(jnp.bitwise_and(tile[2:3, :].astype(i32), LANES - 1).astype(f32))
        here = rows_of(g * LANES, LANES)
        row = weight * (as_column(tile[0:1, :]) - picked[here, :])
        row = jnp.where((lane.astype(i32) == j) & (weight != 0.0), row, 0.0)
        picked[here, :] = row
        back[at, :] = jnp.broadcast_to(jnp.sum(row.T, axis=0, keepdims=True), (TILE, LANES))
        return carry

    lax.fori_loop(0, groups, departures, 0)

    def spread(row, slot):
        at = pl.ds(row, 1)
        forcing[at, :] = forcing[at, :] + picked[pl.ds(slot, 1), :]

    over_rows(spread)
    store.wait()


def kernel_adjoint(
    nlon, nlat, dims, kap, forcing, vel, vc, vs, vn, back,
    middle, hc, hs, hn, got,
    sc, ss, sn, rw, re, rs, rn, sc2, ss2, sn2, rw2, re2, rs2, rn2,
    last, earlier, state, landed, halo_send, halo_recv, row_send, row_recv, local_sem,
):
    nfield, nlevel, nrow = dims
    place = Place(nlon, nlat)
    devices = place.devices
    shared = devices * TILE // back.shape[0]
    nfk = nfield * nlevel
    rows = nfk * nrow
    ctiles = rows // TILE // GROUP
    load_last = pltpu.make_async_copy(forcing.at[pl.ds(2 * rows, rows), :], last, local_sem.at[0])
    load_earlier = pltpu.make_async_copy(
        forcing.at[pl.ds(rows, rows), :], earlier, local_sem.at[1]
    )
    load_last.start()
    load_earlier.start()
    place.hello()
    load_last.wait()
    first = Halo(place, (sc, ss, sn), (rw, re, rs, rn), halo_send.at[0], halo_recv.at[0])
    first.pack_ns(last, 0, nfk, nrow)
    first.pack_ew(last, 0, ctiles)
    place.hello_wait()
    first.start()

    def send_row(i, carry):
        target = lax.rem(place.me + i, devices)
        exchange_copy(
            place, i, tile_at(back, target // shared), tile_at(landed, place.me), row_send, row_recv
        ).start()
        return carry

    lax.fori_loop(1, devices, send_row, 0)
    landed[rows_of(place.me * TILE, TILE), :] = back[rows_of((place.me // shared) * TILE, TILE), :]

    load_earlier.wait()
    first.wait()
    first.finish(nfield, nlevel, False)

    def body(level, carry):
        def at(f):
            return rows_of((f * nlevel + level) * nrow, nrow)

        def put(f, x):
            state[at(f), :] = x

        adjoint_level(
            dims, level, lambda f: last[at(f), :], lambda f: earlier[at(f), :], put,
            vel[at(0), :], vel[at(1), :], kap, first.halos(), (vc, vs, vn),
        )
        return carry

    lax.fori_loop(0, nlevel, body, 0)
    second = Halo(place, (sc2, ss2, sn2), (rw2, re2, rs2, rn2), halo_send.at[1], halo_recv.at[1])
    second.pack_ns(state, 0, nfk, nrow)
    second.pack_ew(state, 0, ctiles)
    second.start()
    keep = pltpu.make_async_copy(state, middle, local_sem.at[2])
    keep.start()

    def wait_row(i, carry):
        source = lax.rem(place.me + devices - i, devices)
        copy = exchange_copy(
            place, i, tile_at(back, 0), tile_at(landed, source), row_send, row_recv
        )
        copy.wait_recv()
        copy.wait_send()
        return carry

    lax.fori_loop(1, devices, wait_row, 0)
    got[...] = landed[...]
    second.wait()
    second.finish(nfield, nlevel, False)
    hc[...] = rw2[...]
    hs[...] = rs2[...]
    hn[...] = rn2[...]
    keep.wait()


def kernel_last(
    nlat, dims, cap, owner, counts, kap, got, slots, hc, hs, hn, vc, vs, vn,
    middle, forcing, vel, adjoint, departures,
):
    nfield, nlevel, nrow = dims
    devices = got.shape[0] // TILE
    shared = LANES // cap
    per = vel.shape[1]
    step = pl.program_id(0)

    @pl.when(step == 0)
    def _():
        me = lax.axis_index("lon") * nlat + lax.axis_index("lat")
        offset = lax.rem(me, shared) * cap
        stack = jnp.concatenate(parts3(got[pl.ds(0, devices, stride=TILE), :]), axis=0)
        i, _ = iotas((LANES, LANES))
        for b in range(owner.shape[0]):
            take = (slots[b : b + 1, :].astype(i32) + offset == i).astype(bf16)
            out = jnp.dot(stack, take, preferred_element_type=f32)
            out = (out[:devices] + out[devices : 2 * devices]) + out[2 * devices :]
            onehot = live_onehot(owner, counts, b, devices)
            departures[b : b + 1, :] = jnp.sum(onehot * out, axis=0, keepdims=True)

    for k in range(per):

        def put(f, x, k=k):
            adjoint[f, k] = x

        adjoint_level(
            dims, step * per + k, lambda f: middle[f, k], lambda f: forcing[0, f, k], put,
            vel[0, k], vel[1, k], kap, (hc, hs, hn), (vc, vs, vn),
        )


def vmem(*shape):
    return jax.ShapeDtypeStruct(shape, f32)


def shards(
    nlon, nlat,
    background, velocity, diffusivity, obs_value, obs_weight, obs_owner, obs_counts, obs_cell,
):
    devices = nlon * nlat
    nfield, nlevel, nrow, ncolumn = background.shape
    nfk = nfield * nlevel
    rows = nfk * nrow
    dims = (nfield, nlevel, nrow)
    nobs = obs_value.shape[0]
    cap = 2 * nobs // devices
    nblock = obs_counts.shape[1]
    ctiles = rows // TILE // GROUP
    vtiles = nlevel * nrow // TILE // GROUP
    groups = devices * cap // LANES
    x0 = background.reshape(rows, LANES)
    vel = velocity.reshape(2 * nlevel * nrow, LANES)
    owner = obs_owner.reshape(nblock, LANES)
    value, weight, cell = [a.reshape(nblock, LANES) for a in (obs_value, obs_weight, obs_cell)]
    in_vmem = pl.BlockSpec(memory_space=pltpu.VMEM)
    in_smem = pl.BlockSpec(memory_space=pltpu.SMEM)
    anywhere = pl.BlockSpec(memory_space=pl.ANY)

    def halo_scratch(columns, edges):
        columns, edges = pltpu.VMEM((columns * TILE, LANES), f32), pltpu.VMEM((edges, LANES), f32)
        return [columns, edges, edges, columns, columns, edges, edges]

    sems = [
        pltpu.SemaphoreType.DMA((2, 5)),
        pltpu.SemaphoreType.DMA((2, 5)),
        pltpu.SemaphoreType.DMA((devices,)),
        pltpu.SemaphoreType.DMA((devices,)),
    ]
    small = halo_scratch(ctiles, nfk)
    large = halo_scratch(ctiles + vtiles, nfk + nlevel)
    whole = pltpu.VMEM((rows, LANES), f32)
    tiles = pltpu.VMEM((devices * TILE, LANES), f32)
    halo_out = [vmem(ctiles * TILE, LANES), vmem(nfk, LANES), vmem(nfk, LANES)]
    vel_halo_out = [vmem(vtiles * TILE, LANES), vmem(nlevel, LANES), vmem(nlevel, LANES)]

    x1, hc, hs, hn, vc, vs, vn, slots, got = pl.pallas_call(
        functools.partial(kernel_forward, nlon, nlat, dims, cap),
        out_shape=[vmem(rows, LANES)]
        + halo_out
        + vel_halo_out
        + [vmem(nblock, LANES), vmem(devices * TILE, LANES)],
        in_specs=[in_vmem, in_smem, in_smem] + [in_vmem] * 5,
        out_specs=[anywhere] + [in_vmem] * 8,
        scratch_shapes=large
        + small
        + [whole, tiles, tiles]
        + sems
        + [pltpu.SemaphoreType.DMA(())],
        compiler_params=pltpu.CompilerParams(
            collective_id=0, has_side_effects=True, vmem_limit_bytes=VMEM_BYTES
        ),
        name="forward",
    )(owner, obs_counts, diffusivity, x0, vel, value, weight, cell)

    x2, forcing, back = pl.pallas_call(
        functools.partial(kernel_rows, devices, dims, cap),
        out_shape=[
            vmem(rows, LANES),
            vmem((STEPS + 1) * rows, LANES),
            vmem(groups * TILE, LANES),
        ],
        in_specs=[in_smem] + [anywhere] * 2 + [in_vmem] * 5,
        out_specs=[anywhere] + [in_vmem] * 2,
        scratch_shapes=[
            pltpu.VMEM(((STEPS + 1) * rows, LANES), f32),
            pltpu.VMEM((groups * LANES, LANES), f32),
            pltpu.VMEM((groups * TILE, LANES), f32),
            pltpu.VMEM((groups, LANES), i32),
            pltpu.VMEM((groups, LANES), i32),
            pltpu.SMEM((groups, LANES), i32),
            pltpu.SMEM((groups, LANES), i32),
            pltpu.SemaphoreType.DMA((5,)),
        ],
        compiler_params=pltpu.CompilerParams(vmem_limit_bytes=VMEM_BYTES),
        name="rows",
    )(diffusivity, x0, x1, vel, hc, hs, hn, got)

    middle, hc, hs, hn, got = pl.pallas_call(
        functools.partial(kernel_adjoint, nlon, nlat, dims),
        out_shape=[vmem(rows, LANES)] + halo_out + [vmem(devices * TILE, LANES)],
        in_specs=[in_smem, anywhere] + [in_vmem] * 5,
        out_specs=[anywhere] + [in_vmem] * 4,
        scratch_shapes=small * 2
        + [whole, whole, whole, tiles]
        + sems
        + [pltpu.SemaphoreType.DMA((3,))],
        compiler_params=pltpu.CompilerParams(
            collective_id=1, has_side_effects=True, vmem_limit_bytes=VMEM_BYTES
        ),
        name="adjoint",
    )(diffusivity, forcing, vel, vc, vs, vn, back)

    shape = background.shape
    per = 4
    block = (nfield, per, nrow, ncolumn)

    def levels(q):
        return (0, q, 0, 0)

    adjoint, departures = pl.pallas_call(
        functools.partial(kernel_last, nlat, dims, cap),
        out_shape=[vmem(*shape), vmem(nblock, LANES)],
        grid=(nlevel // per,),
        in_specs=[in_vmem, in_smem, in_smem]
        + [in_vmem] * 8
        + [
            pl.BlockSpec(block, levels),
            pl.BlockSpec((1,) + block, lambda q: (0, 0, q, 0, 0)),
            pl.BlockSpec((2,) + block[1:], levels),
        ],
        out_specs=[pl.BlockSpec(block, levels), in_vmem],
        compiler_params=pltpu.CompilerParams(vmem_limit_bytes=VMEM_BYTES),
        name="last",
    )(
        owner, obs_counts, diffusivity, got, slots, hc, hs, hn, vc, vs, vn,
        middle.reshape(shape), forcing.reshape((STEPS + 1,) + shape), velocity,
    )
    return x2.reshape(shape), adjoint, departures.reshape(nobs)


def solution(mesh):
    in_specs = (
        P(None, None, "lat", "lon"),
        P(None, None, "lat", "lon"),
        P(),
        P(("lon", "lat")),
        P(("lon", "lat")),
        P(("lon", "lat"), None),
        P(("lon", "lat"), None),
        P(("lon", "lat")),
    )
    out_specs = (P(None, None, "lat", "lon"), P(None, None, "lat", "lon"), P(("lon", "lat")))
    inner = functools.partial(shards, mesh.shape["lon"], mesh.shape["lat"])
    return jax.shard_map(inner, mesh=mesh, in_specs=in_specs, out_specs=out_specs, check_vma=False)
```

```python
import functools

import jax
import jax.numpy as jnp
from jax import lax
from jax.experimental import pallas as pl
from jax.experimental.pallas import tpu as pltpu
from jax.sharding import PartitionSpec as P

STEPS = 2
FLIP_SIGNS = (1.0, 1.0, -1.0, -1.0, 1.0)
LANES = 128
TILE = 8
GROUP = 64
MESH = pl.DeviceIdType.MESH
VMEM_BYTES = 56 * 1024 * 1024
f32 = jnp.float32
bf16 = jnp.bfloat16
i32 = jnp.int32


def rows_of(start, size):
    return pl.ds(pl.multiple_of(start, size), size)


def iotas(shape):
    return lax.broadcasted_iota(i32, shape, 0), lax.broadcasted_iota(i32, shape, 1)


def parts3(x):
    one = x.astype(bf16)
    rest = x - one.astype(f32)
    two = rest.astype(bf16)
    three = (rest - two.astype(f32)).astype(bf16)
    return [one, two, three]


def as_column(row):
    return jnp.broadcast_to(row, (LANES, LANES)).T


class Place:
    def __init__(self, nlon, nlat):
        self.nlon, self.nlat = nlon, nlat
        self.devices = nlon * nlat
        self.lon = lax.axis_index("lon")
        self.lat = lax.axis_index("lat")
        self.me = self.lon * nlat + self.lat
        self.top = self.lat == nlat - 1
        self.bottom = self.lat == 0

    def peer(self, device):
        return (device // self.nlat, lax.rem(device, self.nlat))

    def hello(self):
        barrier = pltpu.get_barrier_semaphore()

        def greet(i, carry):
            other = lax.rem(self.me + i, self.devices)
            pl.semaphore_signal(barrier, inc=1, device_id=self.peer(other), device_id_type=MESH)
            return carry

        lax.fori_loop(1, self.devices, greet, 0)

    def hello_wait(self):
        pl.semaphore_wait(pltpu.get_barrier_semaphore(), self.devices - 1)


class Halo:
    def __init__(self, place, send, recv, send_sem, recv_sem):
        self.place, self.send, self.recv = place, send, recv
        p = place
        west = (lax.rem(p.lon + p.nlon - 1, p.nlon), p.lat)
        east = (lax.rem(p.lon + 1, p.nlon), p.lat)

        def copy(src, dst, k, to):
            return pltpu.make_async_remote_copy(
                src_ref=self.send[src],
                dst_ref=self.recv[dst],
                send_sem=send_sem.at[k],
                recv_sem=recv_sem.at[k],
                device_id=to,
                device_id_type=MESH,
            )

        self.to_west = copy(0, 1, 0, west)
        self.to_east = copy(0, 0, 1, east)
        self.to_south = copy(1, 3, 2, (p.lon, jnp.maximum(p.lat - 1, 0)))
        self.to_north = copy(2, 2, 3, (p.lon, jnp.minimum(p.lat + 1, p.nlat - 1)))
        self.to_fold = copy(2, 3, 4, (p.nlon - 1 - p.lon, p.lat))

    def pack_ns(self, ref, at, count, nrow):
        self.send[1][at : at + count, :] = ref[pl.ds(0, count, stride=nrow), :]
        self.send[2][at : at + count, :] = ref[pl.ds(nrow - 1, count, stride=nrow), :]

    def pack_ew(self, ref, at, tiles):
        _, j = iotas((TILE, LANES))
        owner = jnp.bitwise_and(lax.shift_right_logical(j + 1, 1), GROUP - 1)

        def body(t, carry):
            total = jnp.zeros((TILE, LANES), f32)
            for m in range(GROUP):
                x = ref[rows_of(t * GROUP * TILE + m * TILE, TILE), :]
                x = pltpu.roll(x, 2 * m, 1) if m else x
                total = jnp.where(owner == m, x, total)
            self.send[0][rows_of((at + t) * TILE, TILE), :] = total
            return carry

        lax.fori_loop(0, tiles, body, 0)

    def start(self):
        p = self.place
        self.to_west.start()
        self.to_east.start()

        @pl.when(jnp.logical_not(p.bottom))
        def _():
            self.to_south.start()

        @pl.when(jnp.logical_not(p.top))
        def _():
            self.to_north.start()

        @pl.when(p.top)
        def _():
            self.to_fold.start()

    def wait(self):
        p = self.place
        self.to_west.wait()
        self.to_east.wait()

        @pl.when(jnp.logical_not(p.bottom))
        def _():
            self.to_south.wait_send()
            self.to_north.wait_recv()

        @pl.when(p.bottom)
        def _():
            self.recv[2][...] = jnp.zeros_like(self.recv[2])

        @pl.when(jnp.logical_not(p.top))
        def _():
            self.to_north.wait_send()
            self.to_south.wait_recv()

        @pl.when(p.top)
        def _():
            self.to_fold.wait()

    def finish(self, nfield, nlevel, extra):
        west, east = self.recv[0][...], self.recv[1][...]
        _, j = iotas(west.shape)
        odd = jnp.bitwise_and(j, 1) == 1
        self.recv[0][...] = jnp.where(odd, pltpu.roll(west, 2, 1), east)
        raw = self.recv[3][...]
        i, j = iotas((LANES, LANES))
        turn = (i + j == LANES - 1).astype(bf16)
        a, b, c = [jnp.dot(x, turn, preferred_element_type=f32) for x in parts3(raw)]
        mirrored = (a + b) + c
        signs = [FLIP_SIGNS[k] for k in range(nfield)] + ([-1.0] if extra else [])
        for k, sign in enumerate(signs):
            part = slice(k * nlevel, (k + 1) * nlevel)
            self.recv[3][part, :] = jnp.where(self.place.top, sign * mirrored[part], raw[part])

    def halos(self):
        return self.recv[0], self.recv[2], self.recv[3]


def shifted(x, halos, index, level, nlevel):
    columns, south, north = halos
    nrow = x.shape[0]
    per = nrow // TILE
    first = level * per
    tile = columns[rows_of((index * (nlevel * per // GROUP) + first // GROUP) * TILE, TILE), :]
    turn = LANES - 1 - 2 * lax.rem(first, GROUP)
    z = jnp.concatenate([pltpu.roll(tile, turn - 2 * r, 1) for r in range(per)], axis=0)
    s = south[pl.ds(index * nlevel + level, 1), :]
    n = north[pl.ds(index * nlevel + level, 1), :]
    i, j = iotas(x.shape)
    return (
        jnp.where(j == 0, z, pltpu.roll(x, 1, 1)),
        jnp.where(j == LANES - 1, z, pltpu.roll(x, LANES - 1, 1)),
        jnp.where(i == 0, s, pltpu.roll(x, 1, 0)),
        jnp.where(i == nrow - 1, n, pltpu.roll(x, nrow - 1, 0)),
    )


def forward_step(dims, src, dst, vel, kap, halos):
    nfield, nlevel, nrow = dims

    def body(level, carry):
        u = vel[rows_of(level * nrow, nrow), :]
        v = vel[rows_of((nlevel + level) * nrow, nrow), :]
        speed_u, speed_v = jnp.abs(u), jnp.abs(v)
        for f in range(nfield):
            at = rows_of((f * nlevel + level) * nrow, nrow)
            x = src[at, :]
            w, e, s, n = shifted(x, halos, f, level, nlevel)
            dst[at, :] = (
                x
                + kap[f] * (((e + w) + (n + s)) - 4.0 * x)
                + speed_u * (jnp.where(u < 0.0, e, w) - x)
                + speed_v * (jnp.where(v < 0.0, n, s) - x)
            )
        return carry

    lax.fori_loop(0, nlevel, body, 0, unroll=2)


def adjoint_level(dims, level, src, add, put, u, v, kap, halos, vel_halos):
    nfield, nlevel, nrow = dims
    keep = 1.0 - jnp.abs(u) - jnp.abs(v)
    uw, ue, _, _ = shifted(u, vel_halos, 0, level, nlevel)
    _, _, vs, vn = shifted(v, vel_halos, 0, level, nlevel)
    lw, le = -jnp.minimum(uw, 0.0), jnp.maximum(ue, 0.0)
    ls, ln = -jnp.minimum(vs, 0.0), jnp.maximum(vn, 0.0)
    for f in range(nfield):
        x = src(f)
        w, e, s, n = shifted(x, halos, f, level, nlevel)
        put(
            f,
            (keep * x + add(f))
            + kap[f] * (((e + w) + (n + s)) - 4.0 * x)
            + (lw * w + le * e)
            + (ls * s + ln * n),
        )


def live_onehot(owner, counts, b, devices):
    i, j = iotas((devices, LANES))
    return jnp.where((owner[b : b + 1, :] == i) & (j < counts[0, b]), 1.0, 0.0).astype(f32)


def exchange_copy(place, i, src, dst, send_sem, recv_sem):
    return pltpu.make_async_remote_copy(
        src_ref=src,
        dst_ref=dst,
        send_sem=send_sem.at[i],
        recv_sem=recv_sem.at[i],
        device_id=place.peer(lax.rem(place.me + i, place.devices)),
        device_id_type=MESH,
    )


def tile_at(ref, index):
    return ref.at[rows_of(index * TILE, TILE), :]


def kernel_forward(
    nlon, nlat, dims, cap, owner, counts, kap, x0, vel, value, weight, cell,
    x1, hc, hs, hn, vc, vs, vn, slots, got,
    sc, ss, sn, rw, re, rs, rn, sc2, ss2, sn2, rw2, re2, rs2, rn2,
    state, packed, landed, halo_send, halo_recv, row_send, row_recv, keep_sem,
):
    nfield, nlevel, nrow = dims
    place = Place(nlon, nlat)
    devices = place.devices
    nfk = nfield * nlevel
    ctiles = nfk * nrow // TILE // GROUP
    vtiles = nlevel * nrow // TILE // GROUP
    place.hello()
    first = Halo(place, (sc, ss, sn), (rw, re, rs, rn), halo_send.at[0], halo_recv.at[0])
    first.pack_ns(x0, 0, nfk, nrow)
    first.pack_ns(vel.at[pl.ds(nlevel * nrow, nlevel * nrow), :], nfk, nlevel, nrow)
    first.pack_ew(x0, 0, ctiles)
    first.pack_ew(vel, ctiles, vtiles)
    place.hello_wait()
    first.start()

    nblock = owner.shape[0]
    shared = LANES // cap
    offset = lax.rem(place.me, shared) * cap
    i, j = iotas((LANES, LANES))
    before = (i < j).astype(bf16)
    base = jnp.zeros((devices, 1), f32)
    total = None
    for b in range(nblock):
        onehot = live_onehot(owner, counts, b, devices)
        earlier = jnp.dot(onehot.astype(bf16), before, preferred_element_type=f32)
        slot = jnp.sum(onehot * (earlier + base), axis=0, keepdims=True)
        base = base + jnp.sum(onehot, axis=1, keepdims=True)
        slots[b : b + 1, :] = slot
        code = ((b % (STEPS + 1)) * nfk * nrow * LANES + cell[b : b + 1, :]).astype(f32)
        stack = []
        for data in (value[b : b + 1, :], weight[b : b + 1, :], code):
            stack += parts3(onehot * data)
        place_of = as_column(slot).astype(i32) + offset
        put = (place_of == j).astype(bf16)
        out = jnp.dot(jnp.concatenate(stack, axis=0), put, preferred_element_type=f32)
        total = out if total is None else total + out
    for c in range(3):
        a = total[(3 * c) * devices : (3 * c + 1) * devices]
        a = a + total[(3 * c + 1) * devices : (3 * c + 2) * devices]
        a = a + total[(3 * c + 2) * devices : (3 * c + 3) * devices]
        packed[pl.ds(c, devices, stride=TILE), :] = a
    _, lane = iotas((devices, LANES))
    mine = (lane >= offset) & (lane < offset + cap)
    tally = jnp.where(mine, base, 0.0)
    for c in range(3, TILE):
        packed[pl.ds(c, devices, stride=TILE), :] = tally

    def send_row(i, carry):
        target = lax.rem(place.me + i, devices)
        exchange_copy(
            place, i, tile_at(packed, target), tile_at(landed, place.me), row_send, row_recv
        ).start()
        return carry

    lax.fori_loop(1, devices, send_row, 0)
    landed[rows_of(place.me * TILE, TILE), :] = packed[rows_of(place.me * TILE, TILE), :]

    first.wait()
    first.finish(nfield, nlevel, True)
    forward_step(dims, x0, state, vel, kap, first.halos())
    second = Halo(place, (sc2, ss2, sn2), (rw2, re2, rs2, rn2), halo_send.at[1], halo_recv.at[1])
    second.pack_ns(state, 0, nfk, nrow)
    second.pack_ew(state, 0, ctiles)
    second.start()
    keep = pltpu.make_async_copy(state, x1, keep_sem)
    keep.start()
    vc[...] = rw[ctiles * TILE :, :]
    vs[...] = rs[nfk:, :]
    vn[...] = rn[nfk:, :]

    def wait_row(i, carry):
        source = lax.rem(place.me + devices - i, devices)
        copy = exchange_copy(
            place, i, tile_at(packed, place.me), tile_at(landed, source), row_send, row_recv
        )
        copy.wait_recv()
        copy.wait_send()
        return carry

    lax.fori_loop(1, devices, wait_row, 0)
    got[...] = landed[...]
    second.wait()
    second.finish(nfield, nlevel, False)
    hc[...] = rw2[...]
    hs[...] = rs2[...]
    hn[...] = rn2[...]
    keep.wait()


def kernel_rows(
    devices, dims, cap, kap, x0, x1, vel, hc, hs, hn, got, x2, forcing, back,
    states, picked, tiles, code_v, tally_v, code_s, tally_s, sems,
):
    cells = x0.shape[0]
    shared = LANES // cap
    groups = devices // shared
    loads = []
    for k, x in enumerate((x0, x1)):
        load = pltpu.make_async_copy(x, states.at[pl.ds(k * cells, cells), :], sems.at[k])
        load.start()
        loads.append(load)
    for g in range(groups):
        tile = got[g * shared * TILE : (g * shared + 1) * TILE, :]
        for k in range(1, shared):
            tile = tile + got[(g * shared + k) * TILE : (g * shared + k + 1) * TILE, :]
        tiles[g * TILE : (g + 1) * TILE, :] = tile
        code_v[g : g + 1, :] = tile[2:3, :].astype(i32)
        tally_v[g : g + 1, :] = tile[3:4, :].astype(i32)
    codes = pltpu.make_async_copy(code_v, code_s, sems.at[3])
    tallies = pltpu.make_async_copy(tally_v, tally_s, sems.at[4])
    codes.start()
    tallies.start()

    def clear(i, carry):
        forcing[rows_of(i * LANES, LANES), :] = jnp.zeros((LANES, LANES), f32)
        return carry

    lax.fori_loop(0, forcing.shape[0] // LANES, clear, 0)
    codes.wait()
    tallies.wait()
    for load in loads:
        load.wait()
    newest = states.at[pl.ds(2 * cells, cells), :]
    forward_step(dims, states.at[pl.ds(cells, cells), :], newest, vel, kap, (hc, hs, hn))
    store = pltpu.make_async_copy(newest, x2, sems.at[2])
    store.start()

    def over_rows(visit):
        def source(s, carry):
            g = s // shared
            at = lax.rem(s, shared) * cap

            def chunk(c, inner):
                for k in range(TILE):
                    lane = at + c * TILE + k
                    visit(lax.shift_right_logical(code_s[g, lane], 7), g * LANES + lane)
                return inner

            lax.fori_loop(0, (tally_s[g, at] + TILE - 1) // TILE, chunk, 0)
            return carry

        lax.fori_loop(0, devices, source, 0)

    def pick(row, slot):
        picked[pl.ds(slot, 1), :] = states[pl.ds(row, 1), :]

    over_rows(pick)

    def departures(g, carry):
        at = rows_of(g * TILE, TILE)
        tile = tiles[at, :]
        _, j = iotas((LANES, LANES))
        weight = as_column(tile[1:2, :])
        lane = as_column(jnp.bitwise_and(tile[2:3, :].astype(i32), LANES - 1).astype(f32))
        here = rows_of(g * LANES, LANES)
        row = weight * (as_column(tile[0:1, :]) - picked[here, :])
        row = jnp.where((lane.astype(i32) == j) & (weight != 0.0), row, 0.0)
        picked[here, :] = row
        back[at, :] = jnp.broadcast_to(jnp.sum(row.T, axis=0, keepdims=True), (TILE, LANES))
        return carry

    lax.fori_loop(0, groups, departures, 0)

    def spread(row, slot):
        at = pl.ds(row, 1)
        forcing[at, :] = forcing[at, :] + picked[pl.ds(slot, 1), :]

    over_rows(spread)
    store.wait()


def kernel_adjoint(
    nlon, nlat, dims, kap, forcing, vel, vc, vs, vn, back,
    middle, hc, hs, hn, got,
    sc, ss, sn, rw, re, rs, rn, sc2, ss2, sn2, rw2, re2, rs2, rn2,
    last, earlier, state, landed, halo_send, halo_recv, row_send, row_recv, local_sem,
):
    nfield, nlevel, nrow = dims
    place = Place(nlon, nlat)
    devices = place.devices
    shared = devices * TILE // back.shape[0]
    nfk = nfield * nlevel
    rows = nfk * nrow
    ctiles = rows // TILE // GROUP
    load_last = pltpu.make_async_copy(forcing.at[pl.ds(2 * rows, rows), :], last, local_sem.at[0])
    load_earlier = pltpu.make_async_copy(
        forcing.at[pl.ds(rows, rows), :], earlier, local_sem.at[1]
    )
    load_last.start()
    load_earlier.start()
    place.hello()
    load_last.wait()
    first = Halo(place, (sc, ss, sn), (rw, re, rs, rn), halo_send.at[0], halo_recv.at[0])
    first.pack_ns(last, 0, nfk, nrow)
    first.pack_ew(last, 0, ctiles)
    place.hello_wait()
    first.start()

    def send_row(i, carry):
        target = lax.rem(place.me + i, devices)
        exchange_copy(
            place, i, tile_at(back, target // shared), tile_at(landed, place.me), row_send, row_recv
        ).start()
        return carry

    lax.fori_loop(1, devices, send_row, 0)
    landed[rows_of(place.me * TILE, TILE), :] = back[rows_of((place.me // shared) * TILE, TILE), :]

    load_earlier.wait()
    first.wait()
    first.finish(nfield, nlevel, False)

    def body(level, carry):
        def at(f):
            return rows_of((f * nlevel + level) * nrow, nrow)

        def put(f, x):
            state[at(f), :] = x

        adjoint_level(
            dims, level, lambda f: last[at(f), :], lambda f: earlier[at(f), :], put,
            vel[at(0), :], vel[at(1), :], kap, first.halos(), (vc, vs, vn),
        )
        return carry

    lax.fori_loop(0, nlevel, body, 0, unroll=2)
    second = Halo(place, (sc2, ss2, sn2), (rw2, re2, rs2, rn2), halo_send.at[1], halo_recv.at[1])
    second.pack_ns(state, 0, nfk, nrow)
    second.pack_ew(state, 0, ctiles)
    second.start()
    keep = pltpu.make_async_copy(state, middle, local_sem.at[2])
    keep.start()

    def wait_row(i, carry):
        source = lax.rem(place.me + devices - i, devices)
        copy = exchange_copy(
            place, i, tile_at(back, 0), tile_at(landed, source), row_send, row_recv
        )
        copy.wait_recv()
        copy.wait_send()
        return carry

    lax.fori_loop(1, devices, wait_row, 0)
    got[...] = landed[...]
    second.wait()
    second.finish(nfield, nlevel, False)
    hc[...] = rw2[...]
    hs[...] = rs2[...]
    hn[...] = rn2[...]
    keep.wait()


def kernel_last(
    nlat, dims, cap, owner, counts, kap, got, slots, hc, hs, hn, vc, vs, vn,
    middle, forcing, vel, adjoint, departures,
):
    nfield, nlevel, nrow = dims
    devices = got.shape[0] // TILE
    shared = LANES // cap
    per = vel.shape[1]
    step = pl.program_id(0)

    @pl.when(step == 0)
    def _():
        me = lax.axis_index("lon") * nlat + lax.axis_index("lat")
        offset = lax.rem(me, shared) * cap
        stack = jnp.concatenate(parts3(got[pl.ds(0, devices, stride=TILE), :]), axis=0)
        i, _ = iotas((LANES, LANES))
        for b in range(owner.shape[0]):
            take = (slots[b : b + 1, :].astype(i32) + offset == i).astype(bf16)
            out = jnp.dot(stack, take, preferred_element_type=f32)
            out = (out[:devices] + out[devices : 2 * devices]) + out[2 * devices :]
            onehot = live_onehot(owner, counts, b, devices)
            departures[b : b + 1, :] = jnp.sum(onehot * out, axis=0, keepdims=True)

    for k in range(per):

        def put(f, x, k=k):
            adjoint[f, k] = x

        adjoint_level(
            dims, step * per + k, lambda f: middle[f, k], lambda f: forcing[0, f, k], put,
            vel[0, k], vel[1, k], kap, (hc, hs, hn), (vc, vs, vn),
        )


def vmem(*shape):
    return jax.ShapeDtypeStruct(shape, f32)


def shards(
    nlon, nlat,
    background, velocity, diffusivity, obs_value, obs_weight, obs_owner, obs_counts, obs_cell,
):
    devices = nlon * nlat
    nfield, nlevel, nrow, ncolumn = background.shape
    nfk = nfield * nlevel
    rows = nfk * nrow
    dims = (nfield, nlevel, nrow)
    nobs = obs_value.shape[0]
    cap = 2 * nobs // devices
    nblock = obs_counts.shape[1]
    ctiles = rows // TILE // GROUP
    vtiles = nlevel * nrow // TILE // GROUP
    groups = devices * cap // LANES
    x0 = background.reshape(rows, LANES)
    vel = velocity.reshape(2 * nlevel * nrow, LANES)
    owner = obs_owner.reshape(nblock, LANES)
    value, weight, cell = [a.reshape(nblock, LANES) for a in (obs_value, obs_weight, obs_cell)]
    in_vmem = pl.BlockSpec(memory_space=pltpu.VMEM)
    in_smem = pl.BlockSpec(memory_space=pltpu.SMEM)
    anywhere = pl.BlockSpec(memory_space=pl.ANY)

    def halo_scratch(columns, edges):
        columns, edges = pltpu.VMEM((columns * TILE, LANES), f32), pltpu.VMEM((edges, LANES), f32)
        return [columns, edges, edges, columns, columns, edges, edges]

    sems = [
        pltpu.SemaphoreType.DMA((2, 5)),
        pltpu.SemaphoreType.DMA((2, 5)),
        pltpu.SemaphoreType.DMA((devices,)),
        pltpu.SemaphoreType.DMA((devices,)),
    ]
    small = halo_scratch(ctiles, nfk)
    large = halo_scratch(ctiles + vtiles, nfk + nlevel)
    whole = pltpu.VMEM((rows, LANES), f32)
    tiles = pltpu.VMEM((devices * TILE, LANES), f32)
    halo_out = [vmem(ctiles * TILE, LANES), vmem(nfk, LANES), vmem(nfk, LANES)]
    vel_halo_out = [vmem(vtiles * TILE, LANES), vmem(nlevel, LANES), vmem(nlevel, LANES)]

    x1, hc, hs, hn, vc, vs, vn, slots, got = pl.pallas_call(
        functools.partial(kernel_forward, nlon, nlat, dims, cap),
        out_shape=[vmem(rows, LANES)]
        + halo_out
        + vel_halo_out
        + [vmem(nblock, LANES), vmem(devices * TILE, LANES)],
        in_specs=[in_vmem, in_smem, in_smem] + [in_vmem] * 5,
        out_specs=[anywhere] + [in_vmem] * 8,
        scratch_shapes=large
        + small
        + [whole, tiles, tiles]
        + sems
        + [pltpu.SemaphoreType.DMA(())],
        compiler_params=pltpu.CompilerParams(
            collective_id=0, has_side_effects=True, vmem_limit_bytes=VMEM_BYTES
        ),
        name="forward",
    )(owner, obs_counts, diffusivity, x0, vel, value, weight, cell)

    x2, forcing, back = pl.pallas_call(
        functools.partial(kernel_rows, devices, dims, cap),
        out_shape=[
            vmem(rows, LANES),
            vmem((STEPS + 1) * rows, LANES),
            vmem(groups * TILE, LANES),
        ],
        in_specs=[in_smem] + [anywhere] * 2 + [in_vmem] * 5,
        out_specs=[anywhere] + [in_vmem] * 2,
        scratch_shapes=[
            pltpu.VMEM(((STEPS + 1) * rows, LANES), f32),
            pltpu.VMEM((groups * LANES, LANES), f32),
            pltpu.VMEM((groups * TILE, LANES), f32),
            pltpu.VMEM((groups, LANES), i32),
            pltpu.VMEM((groups, LANES), i32),
            pltpu.SMEM((groups, LANES), i32),
            pltpu.SMEM((groups, LANES), i32),
            pltpu.SemaphoreType.DMA((5,)),
        ],
        compiler_params=pltpu.CompilerParams(vmem_limit_bytes=VMEM_BYTES),
        name="rows",
    )(diffusivity, x0, x1, vel, hc, hs, hn, got)

    middle, hc, hs, hn, got = pl.pallas_call(
        functools.partial(kernel_adjoint, nlon, nlat, dims),
        out_shape=[vmem(rows, LANES)] + halo_out + [vmem(devices * TILE, LANES)],
        in_specs=[in_smem, anywhere] + [in_vmem] * 5,
        out_specs=[anywhere] + [in_vmem] * 4,
        scratch_shapes=small * 2
        + [whole, whole, whole, tiles]
        + sems
        + [pltpu.SemaphoreType.DMA((3,))],
        compiler_params=pltpu.CompilerParams(
            collective_id=1, has_side_effects=True, vmem_limit_bytes=VMEM_BYTES
        ),
        name="adjoint",
    )(diffusivity, forcing, vel, vc, vs, vn, back)

    shape = background.shape
    per = 4
    block = (nfield, per, nrow, ncolumn)

    def levels(q):
        return (0, q, 0, 0)

    adjoint, departures = pl.pallas_call(
        functools.partial(kernel_last, nlat, dims, cap),
        out_shape=[vmem(*shape), vmem(nblock, LANES)],
        grid=(nlevel // per,),
        in_specs=[in_vmem, in_smem, in_smem]
        + [in_vmem] * 8
        + [
            pl.BlockSpec(block, levels),
            pl.BlockSpec((1,) + block, lambda q: (0, 0, q, 0, 0)),
            pl.BlockSpec((2,) + block[1:], levels),
        ],
        out_specs=[pl.BlockSpec(block, levels), in_vmem],
        compiler_params=pltpu.CompilerParams(vmem_limit_bytes=VMEM_BYTES),
        name="last",
    )(
        owner, obs_counts, diffusivity, got, slots, hc, hs, hn, vc, vs, vn,
        middle.reshape(shape), forcing.reshape((STEPS + 1,) + shape), velocity,
    )
    return x2.reshape(shape), adjoint, departures.reshape(nobs)


def solution(mesh):
    in_specs = (
        P(None, None, "lat", "lon"),
        P(None, None, "lat", "lon"),
        P(),
        P(("lon", "lat")),
        P(("lon", "lat")),
        P(("lon", "lat"), None),
        P(("lon", "lat"), None),
        P(("lon", "lat")),
    )
    out_specs = (P(None, None, "lat", "lon"), P(None, None, "lat", "lon"), P(("lon", "lat")))
    inner = functools.partial(shards, mesh.shape["lon"], mesh.shape["lat"])
    return jax.shard_map(inner, mesh=mesh, in_specs=in_specs, out_specs=out_specs, check_vma=False)
```
